512 devices in a mesh: section: 16 (over y_hi, x, core), dp: 4 (over y_lo), mp: 8 (over z).
Axes of the slice: x: 4, y: 8 (y_hi: 2, y_lo: 4; y = y_hi * 4 + y_lo), z: 8, core: 2. Of those that a mesh axis runs over, the one named last changes fastest.
Arguments:
- token_ids: int32 [16384], P(('section', 'dp')), may hold values from 0 to 127999, as said below
- table: bfloat16 [128000, 4608], P(('section', 'dp'), 'mp')
- norm_weight: float32 [4608], P('mp'), may hold values from -0.5 to 0.5
- cotangent: bfloat16 [16384, 4608], P(('section', 'dp'), 'mp')
Outputs:
- normed: bfloat16 [16384, 4608], P(('section', 'dp'), 'mp')
- weight_grad: float32 [4608], P('mp')
- table_grad: bfloat16 [128000, 4608], P(('section', 'dp'), 'mp')
The draws below stay inside these ranges and needn't reach their ends.
Inputs may be any that keep to these rules, and one draw needn't show every extreme that they name: Owner j holds ids j * 2000 to (j + 1) * 2000 - 1. Among the 256 tokens of one device (aligned blocks of token_ids), at most 8 ids fall in any one owner's block; in every draw one owner receives exactly 8 ids from every device.
All inputs are finite; a program needn't handle non-finite values.
Results may differ from the reference program's by a relative error of at most 0.0026.
Values may be sent and summed in bfloat16 or wider, within the bound.
A program may use at most 64 MiB of HBM per device.

```python
import math
import jax
import jax.numpy as jnp
from jax import lax

D = 4608
VOCAB = 128000
TOK_DEV = 256
OWNERS = 64
VROWS = 2000
CAP = 8
TOKENS = 16384


def draw_token_ids(key, part):
    key = jax.random.fold_in(key, 5)
    first, second = jax.random.split(key, 2)
    full_owner = jax.random.randint(first, (), 0, OWNERS).astype(jnp.int32)

    def one_block(block_key):
        order_key, mix_key, offset_key = jax.random.split(block_key, 3)
        order = jax.random.permutation(order_key, (OWNERS - 1) * CAP)[:TOK_DEV - CAP]
        other = (order // CAP).astype(jnp.int32)
        other = other + (other >= full_owner).astype(jnp.int32)
        chosen = jnp.concatenate([jnp.full((CAP,), 0, jnp.int32) + full_owner, other])
        chosen = jax.random.permutation(mix_key, chosen)
        offset = jax.random.randint(offset_key, (TOK_DEV,), 0, VROWS).astype(jnp.int32)
        return chosen * VROWS + offset
    block_keys = jax.random.split(second, OWNERS)
    return jax.vmap(one_block)(block_keys).reshape(TOKENS).astype(jnp.int32)


def draw_table(key, part):
    key = jax.random.fold_in(key, 11)
    first, second, third = jax.random.split(key, 3)
    base = jnp.clip(jax.random.normal(first, (VOCAB, D), jnp.float32), -4.0, 4.0)
    row_scale = jnp.exp(math.log(10.0) * jax.random.uniform(second, (VOCAB, 1), jnp.float32))
    rise = jnp.exp(math.log(3.0) * jnp.arange(D, dtype=jnp.float32) / D)
    col_scale = jnp.exp(math.log(10.0) * jax.random.uniform(third, (1, D), jnp.float32)) * rise[None, :]
    return (0.1 * base * row_scale * col_scale).astype(jnp.bfloat16)


def draw_cotangent(key, part):
    key = jax.random.fold_in(key, 23)
    first, second, third = jax.random.split(key, 3)
    base = jnp.clip(jax.random.normal(first, (TOKENS, D), jnp.float32), -4.0, 4.0)
    token_scale = jnp.exp(math.log(10.0) * jax.random.uniform(second, (TOKENS, 1), jnp.float32))
    rise = jnp.exp(math.log(3.0) * jnp.arange(TOKENS, dtype=jnp.float32) / TOKENS)
    col_scale = jnp.exp(math.log(10.0) * jax.random.uniform(third, (1, D), jnp.float32))
    return (0.1 * base * token_scale * rise[:, None] * col_scale).astype(jnp.bfloat16)


def steps_of(stream_key, shape, cuts, smallest, top_value):
    def one(dim, blocks):
        steps = jax.random.uniform(jax.random.fold_in(jax.random.fold_in(stream_key, 6), dim), (blocks,), jnp.float32, smallest / len(cuts), top_value / len(cuts))
        return jnp.repeat(jnp.exp(steps), shape[dim] // blocks).reshape((-1,) + (1,) * (len(shape) - dim - 1))

    level = one(*cuts[0])
    for cut in cuts[1:]:
        level = level * one(*cut)
    return level


def setup_inputs(seed: int = 0) -> dict:
    keys = jax.random.split(jax.random.key(seed), 5)
    token_ids = draw_token_ids(jax.random.fold_in(keys[4], 71), 0)
    table = draw_table(jax.random.fold_in(keys[4], 71), 0)
    norm_weight = jnp.clip(jax.random.uniform(keys[2], (D,), jnp.float32, -0.5, 0.5) * steps_of(keys[2], (D,), ((0, 8),), -0.4, 0.0), -0.5, 0.5)
    cotangent = draw_cotangent(jax.random.fold_in(keys[4], 71), 0)
    return {"token_ids": token_ids, "table": table, "norm_weight": norm_weight, "cotangent": cotangent}


column_blocks = 8

def reference(token_ids, table, norm_weight, cotangent):
    embedded = jnp.take(table, token_ids, axis=0)
    scale = math.sqrt(D)
    scaled = embedded.astype(jnp.float32) * scale
    inv_rms = lax.rsqrt(lax.optimization_barrier(jnp.mean(scaled * scaled, axis=1)) + 1e-06)
    unit = scaled * inv_rms[:, None]
    multiplier = 1.0 + norm_weight.astype(jnp.float32)
    normed = (unit * multiplier[None, :]).astype(jnp.bfloat16)
    incoming = cotangent.astype(jnp.float32)
    weight_grad = lax.optimization_barrier(jnp.sum(incoming * unit, axis=0))
    grad_hat = incoming * multiplier[None, :]
    inner = lax.optimization_barrier(jnp.mean(grad_hat * unit, axis=1))
    grad_embed = (scale * inv_rms[:, None] * (grad_hat - unit * inner[:, None])).astype(jnp.bfloat16)
    blocks = grad_embed.astype(jnp.float32).reshape(TOKENS, column_blocks, D // column_blocks).transpose(1, 0, 2)

    def accumulate(block):
        return jax.ops.segment_sum(block, token_ids, num_segments=VOCAB).astype(jnp.bfloat16)
    summed = lax.map(accumulate, blocks)
    table_grad = summed.transpose(1, 0, 2).reshape(VOCAB, D)
    return (normed, weight_grad, table_grad)
```

```python
import functools
import math

import jax
import jax.numpy as jnp
from jax import lax
from jax.experimental import pallas as pl
from jax.experimental.pallas import tpu as pltpu
from jax.sharding import PartitionSpec as P

MESH = pl.DeviceIdType.MESH
F32 = jnp.float32
BF16 = jnp.bfloat16
EPS = 1e-06
NT = (((1,), (1,)), ((), ()))
TN = (((0,), (0,)), ((), ()))

CHUNK = 128


def kernel(
    dims,
    ids_ref,
    weight_ref,
    cot_ref,
    table_hbm,
    normed_ref,
    wg_ref,
    grad_hbm,
    table_ref,
    ext_ref,
    place_ref,
    send_ref,
    recv_ref,
    hot_ref,
    rows_ref,
    part_ref,
    zbuf_ref,
    back_ref,
    done_ref,
    g_ref,
    grad_ref,
    wgp_ref,
    wg1_ref,
    wgs_ref,
    wg2_ref,
    sems,
):
    groups, ring, cap, cores = dims
    owners = lax.axis_size("section") * groups
    heights = owners // cores
    width, count = cot_ref.shape
    vrows = table_ref.shape[1]
    slots = owners * cap
    scale = math.sqrt(width * ring)
    chunks = slots // CHUNK
    per = CHUNK // cap

    sec = lax.axis_index("section")
    grp = lax.axis_index("dp")
    col = lax.axis_index("mp")
    me = sec * groups + grp
    inner_id = lax.rem(sec, cores)
    height = lax.div(sec, cores) * groups + grp

    def plane(step):
        p = lax.rem(me + step, owners)
        return p, (lax.div(p, groups), lax.rem(p, groups), col)

    def along(step):
        return (sec, grp, lax.rem(col + step, ring))

    def beside(step):
        return (sec - inner_id + lax.rem(inner_id + step, cores), grp, col)

    def above(step):
        h = lax.rem(height + step, heights)
        return (lax.div(h, groups) * cores + inner_id, lax.rem(h, groups), col)

    barrier = pltpu.get_barrier_semaphore()

    @pl.loop(1, owners)
    def _(k):
        pl.semaphore_signal(barrier, inc=1, device_id=plane(k)[1], device_id_type=MESH)

    @pl.loop(1, ring)
    def _(k):
        pl.semaphore_signal(barrier, inc=1, device_id=along(k), device_id_type=MESH)

    table_copy = pltpu.make_async_copy(table_hbm, table_ref, sems.at[0])
    table_copy.start()

    ids = jnp.broadcast_to(ids_ref[...], (owners, count))
    local = ids - vrows * lax.broadcasted_iota(jnp.int32, (owners, count), 0)
    member = (local >= 0) & (local < vrows)
    before = lax.broadcasted_iota(jnp.int32, (count, count), 0) < lax.broadcasted_iota(
        jnp.int32, (count, count), 1
    )
    rank = jnp.dot(
        jnp.where(member, 1.0, 0.0).astype(BF16),
        jnp.where(before, 1.0, 0.0).astype(BF16),
        preferred_element_type=F32,
    )
    rank = jnp.where(member, rank, -1.0)
    slot_of = lax.broadcasted_iota(jnp.int32, (owners, cap, count), 1).astype(F32)
    place = jnp.where(rank[:, None, :] == slot_of, 1.0, 0.0).reshape(slots, count)
    place_ref[...] = place.astype(BF16)
    within = jnp.sum(jnp.where(member, local, 0), axis=0, keepdims=True)
    extra = ext_ref.shape[0] - width
    within = jnp.broadcast_to(within, (extra, count))
    line = lax.broadcasted_iota(jnp.int32, (extra, count), 0)
    code = jnp.where(line == 0, (within >> 6) + 1, jnp.where(line == 1, within & 63, 0))
    ext_ref[:width, :] = cot_ref[...]
    ext_ref[width:, :] = code.astype(F32).astype(BF16)
    for q in range(chunks):
        packed = lax.dot_general(
            place_ref[q * CHUNK : (q + 1) * CHUNK, :], ext_ref[...], NT, preferred_element_type=F32
        )
        send_ref[q * per : (q + 1) * per] = packed.reshape(per, cap, -1).astype(BF16)

    pl.semaphore_wait(barrier, owners - 1 + ring - 1)

    def exchange(src, dst, send_sem, recv_sem):
        @pl.loop(1, owners)
        def _(k):
            p, device = plane(k)
            pltpu.make_async_remote_copy(
                src_ref=src.at[p],
                dst_ref=dst.at[me],
                send_sem=send_sem,
                recv_sem=recv_sem,
                device_id=device,
                device_id_type=MESH,
            ).start()

    def wait_blocks(ref, number, sem):
        part = ref.at[pl.ds(0, number)]
        pltpu.make_async_copy(part, part, sem).wait()

    exchange(send_ref, recv_ref, sems.at[1], sems.at[2])
    recv_ref[me] = send_ref[me]
    table_copy.wait()
    multiplier = 1.0 + weight_ref[...]
    wait_blocks(recv_ref, owners - 1, sems.at[2])

    def received(q):
        block = recv_ref[q * per : (q + 1) * per].astype(F32)
        return block.reshape(CHUNK, block.shape[2])

    lane = lax.broadcasted_iota(jnp.int32, (CHUNK, 128), 1)
    for q in range(chunks):
        here = slice(q * CHUNK, (q + 1) * CHUNK)
        block = received(q)
        wanted = (block[:, width : width + 1] - 1.0) * 64.0 + block[:, width + 1 : width + 2]
        entry = lax.broadcasted_iota(jnp.int32, (CHUNK, vrows), 1).astype(F32)
        hot_ref[here, :] = jnp.where(wanted == entry, 1.0, 0.0).astype(BF16)
        rows = lax.dot_general(
            hot_ref[here, :], table_ref[...], NT, preferred_element_type=F32
        )
        rows_ref[here, :] = rows
        squares = jnp.sum(rows * rows, axis=1, keepdims=True)
        near = lax.rsqrt(squares + EPS)
        product = jnp.sum(block[:, :width] * multiplier * (rows * near), axis=1, keepdims=True)
        both = jnp.where(lane == 0, squares, jnp.where(lane == 1, product, 0.0)).T
        part_ref[q : q + 1, :] = both[0:1, :]
        part_ref[chunks + q : chunks + q + 1, :] = both[1:2, :]

    @pl.loop(1, ring)
    def _(k):
        pltpu.make_async_remote_copy(
            src_ref=part_ref,
            dst_ref=zbuf_ref.at[col],
            send_sem=sems.at[3],
            recv_sem=sems.at[4],
            device_id=along(k),
            device_id_type=MESH,
        ).start()

    zbuf_ref[col] = part_ref[...]
    wait_blocks(zbuf_ref, ring - 1, sems.at[4])

    squares = jnp.zeros((chunks, 128), F32)
    product = jnp.zeros((chunks, 128), F32)
    for z in range(ring):
        theirs = zbuf_ref[z, :chunks, :]
        squares += theirs
        product += zbuf_ref[z, chunks:, :] / lax.rsqrt(theirs + EPS)
    inverse = lax.rsqrt(squares + EPS)
    product = product * inverse * (scale / (width * ring))
    columns = jnp.concatenate(
        [inverse, product, jnp.zeros((128 - 2 * chunks, 128), F32)], axis=0
    ).T
    total = jnp.zeros((1, width), F32)
    for q in range(chunks):
        here = slice(q * CHUNK, (q + 1) * CHUNK)
        inv_rms = columns[:, q : q + 1]
        inner = columns[:, chunks + q : chunks + q + 1]
        incoming = received(q)[:, :width]
        unit = rows_ref[here, :] * scale * inv_rms
        normed = unit * multiplier
        back_ref[q * per : (q + 1) * per, :, :width] = normed.reshape(per, cap, width).astype(BF16)
        total += jnp.sum(incoming * unit, axis=0, keepdims=True)
        grad_hat = incoming * multiplier
        g_ref[here, :] = (scale * inv_rms * (grad_hat - unit * inner)).astype(BF16)
    back_ref[:, :, width:] = jnp.zeros((owners, cap, extra), BF16)

    wgp_ref[:, :width] = total
    wgp_ref[:, width:] = jnp.zeros((1, extra), F32)

    def gather_sum(src, dst, mine, number, device_of, send_sem, recv_sem):
        @pl.loop(1, number)
        def _(k):
            pltpu.make_async_remote_copy(
                src_ref=src,
                dst_ref=dst.at[mine],
                send_sem=send_sem,
                recv_sem=recv_sem,
                device_id=device_of(k),
                device_id_type=MESH,
            ).start()

        dst[mine] = src[...]

    gather_sum(wgp_ref, wg1_ref, inner_id, cores, beside, sems.at[5], sems.at[6])
    exchange(back_ref, done_ref, sems.at[7], sems.at[8])
    done_ref[me] = back_ref[me]
    wait_blocks(wg1_ref, cores - 1, sems.at[6])
    wgs_ref[...] = jnp.sum(wg1_ref[...], axis=0)
    gather_sum(wgs_ref, wg2_ref, height, heights, above, sems.at[9], sems.at[10])

    grad_ref[...] = lax.dot_general(
        g_ref[...], hot_ref[...], TN, preferred_element_type=F32
    ).astype(BF16)
    grad_copy = pltpu.make_async_copy(grad_ref, grad_hbm, sems.at[0])
    grad_copy.start()

    wait_blocks(wg2_ref, heights - 1, sems.at[10])
    wg_ref[...] = jnp.sum(wg2_ref[...], axis=0)[:, :width]
    wait_blocks(done_ref, owners - 1, sems.at[8])
    arrived = done_ref[...].astype(F32).reshape(slots, done_ref.shape[2])[:, :width].astype(BF16)
    normed_ref[...] = lax.dot_general(
        arrived, place_ref[...], TN, preferred_element_type=F32
    ).astype(BF16)

    wait_blocks(send_ref, owners - 1, sems.at[1])
    wait_blocks(zbuf_ref, ring - 1, sems.at[3])
    wait_blocks(wg1_ref, cores - 1, sems.at[5])
    wait_blocks(back_ref, owners - 1, sems.at[7])
    wait_blocks(wg2_ref, heights - 1, sems.at[9])
    grad_copy.wait()


def body(mesh, token_ids, table, norm_weight, cotangent):
    groups, ring = mesh.shape["dp"], mesh.shape["mp"]
    owners = mesh.shape["section"] * groups
    vrows, width = table.shape
    count = token_ids.shape[0]
    cap = 2 * count // owners
    cores = 8
    heights = owners // cores
    slots = owners * cap
    wide = -(-(width + 2) // 128) * 128
    vmem = pl.BlockSpec(memory_space=pltpu.VMEM)
    hbm = pl.BlockSpec(memory_space=pl.ANY)
    normed, weight_grad, table_grad = pl.pallas_call(
        functools.partial(kernel, (groups, ring, cap, cores)),
        out_shape=(
            jax.ShapeDtypeStruct((width, count), BF16),
            jax.ShapeDtypeStruct((1, width), F32),
            jax.ShapeDtypeStruct((width, vrows), BF16),
        ),
        in_specs=[vmem, vmem, vmem, hbm],
        out_specs=(vmem, vmem, hbm),
        scratch_shapes=[
            pltpu.VMEM((width, vrows), BF16),
            pltpu.VMEM((wide, count), BF16),
            pltpu.VMEM((slots, count), BF16),
            pltpu.VMEM((owners, cap, wide), BF16),
            pltpu.VMEM((owners, cap, wide), BF16),
            pltpu.VMEM((slots, vrows), BF16),
            pltpu.VMEM((slots, width), F32),
            pltpu.VMEM((2 * slots // CHUNK, 128), F32),
            pltpu.VMEM((ring, 2 * slots // CHUNK, 128), F32),
            pltpu.VMEM((owners, cap, wide), BF16),
            pltpu.VMEM((owners, cap, wide), BF16),
            pltpu.VMEM((slots, width), BF16),
            pltpu.VMEM((width, vrows), BF16),
            pltpu.VMEM((1, wide), F32),
            pltpu.VMEM((cores, 1, wide), F32),
            pltpu.VMEM((1, wide), F32),
            pltpu.VMEM((heights, 1, wide), F32),
            pltpu.SemaphoreType.DMA((11,)),
        ],
        compiler_params=pltpu.CompilerParams(
            collective_id=0, has_side_effects=True, vmem_limit_bytes=40 * 1024 * 1024
        ),
    )(token_ids.reshape(1, count), norm_weight.reshape(1, width), cotangent.T, table.T)
    return normed.T, weight_grad.reshape(width), table_grad.T


def solution(mesh):
    placed = (P(("section", "dp")), P(("section", "dp"), "mp"), P("mp"), P(("section", "dp"), "mp"))
    return jax.shard_map(
        functools.partial(body, mesh),
        mesh=mesh,
        in_specs=placed,
        out_specs=(P(("section", "dp"), "mp"), P("mp"), P(("section", "dp"), "mp")),
        check_vma=False,
    )
```

```python
import functools
import math

import jax
import jax.numpy as jnp
from jax import lax
from jax.experimental import pallas as pl
from jax.experimental.pallas import tpu as pltpu
from jax.sharding import PartitionSpec as P

MESH = pl.DeviceIdType.MESH
F32 = jnp.float32
BF16 = jnp.bfloat16
EPS = 1e-06
NT = (((1,), (1,)), ((), ()))
TN = (((0,), (0,)), ((), ()))

CHUNK = 128


def kernel(
    dims,
    ids_hbm,
    weight_hbm,
    cot_hbm,
    table_hbm,
    normed_ref,
    wg_ref,
    grad_ref,
    ids_ref,
    weight_ref,
    table_ref,
    cot_ref,
    place_ref,
    ask_ref,
    asked_ref,
    send_ref,
    recv_ref,
    hot_ref,
    unit_ref,
    part_ref,
    square_ref,
    inner_ref,
    back_ref,
    done_ref,
    g_ref,
    wgp_ref,
    wg1_ref,
    wgs_ref,
    wg2_ref,
    local_sems,
    send_sems,
    recv_sems,
):
    groups, ring, cap, cores = dims
    owners = lax.axis_size("section") * groups
    heights = owners // cores
    width, count = cot_ref.shape
    vrows = table_ref.shape[1]
    slots = owners * cap
    wide = send_ref.shape[2]
    scale = math.sqrt(width * ring)
    chunks = slots // CHUNK
    per = CHUNK // cap

    sec = lax.axis_index("section")
    grp = lax.axis_index("dp")
    col = lax.axis_index("mp")
    me = sec * groups + grp
    inner_id = lax.rem(sec, cores)
    height = lax.div(sec, cores) * groups + grp

    def plane(step):
        p = lax.rem(me + step, owners)
        return p, (lax.div(p, groups), lax.rem(p, groups), col)

    def along(step):
        return (sec, grp, lax.rem(col + step, ring))

    def beside(step):
        return (sec - inner_id + lax.rem(inner_id + step, cores), grp, col)

    def above(step):
        h = lax.rem(height + step, heights)
        return (lax.div(h, groups) * cores + inner_id, lax.rem(h, groups), col)

    barrier = pltpu.get_barrier_semaphore()

    @pl.loop(1, owners)
    def _(k):
        pl.semaphore_signal(barrier, inc=1, device_id=plane(k)[1], device_id_type=MESH)

    @pl.loop(1, ring)
    def _(k):
        pl.semaphore_signal(barrier, inc=1, device_id=along(k), device_id_type=MESH)

    fetches = [
        pltpu.make_async_copy(src, dst, local_sems.at[n])
        for n, (src, dst) in enumerate(
            (
                (ids_hbm, ids_ref),
                (cot_hbm, cot_ref),
                (weight_hbm, weight_ref),
                (table_hbm, table_ref),
            )
        )
    ]
    for fetch in fetches:
        fetch.start()

    before = lax.broadcasted_iota(jnp.int32, (count, count), 0) < lax.broadcasted_iota(
        jnp.int32, (count, count), 1
    )
    before = jnp.where(before, 1.0, 0.0).astype(BF16)
    fetches[0].wait()
    ids = jnp.broadcast_to(ids_ref[...], (owners, count))
    local = ids - vrows * lax.broadcasted_iota(jnp.int32, (owners, count), 0)
    member = (local >= 0) & (local < vrows)
    rank = jnp.dot(
        jnp.where(member, 1.0, 0.0).astype(BF16), before, preferred_element_type=F32
    )
    rank = jnp.where(member, rank, -1.0)
    lane = lax.broadcasted_iota(jnp.int32, (owners, 128), 1)
    wanted = jnp.full((owners, 128), -1, jnp.int32)
    for s in range(cap):
        one = jnp.sum(jnp.where(rank == s, local + 1, 0), axis=1, keepdims=True) - 1
        wanted = jnp.where(lane == s, one, wanted)
    ask_ref[...] = wanted[:, None, :]
    slot_of = lax.broadcasted_iota(jnp.int32, (owners, cap, count), 1).astype(F32)
    place = jnp.where(rank[:, None, :] == slot_of, 1.0, 0.0).reshape(slots, count)
    place_ref[...] = place.astype(BF16)

    def send_to(src, dst, n, device):
        pltpu.make_async_remote_copy(
            src_ref=src,
            dst_ref=dst,
            send_sem=send_sems.at[n],
            recv_sem=recv_sems.at[n],
            device_id=device,
            device_id_type=MESH,
        ).start()

    def exchange(src, dst, n):
        @pl.loop(1, owners)
        def _(k):
            p, device = plane(k)
            send_to(src.at[p], dst.at[me], n, device)

    def share(src, dst, n, mine, number, device_of):
        @pl.loop(1, number)
        def _(k):
            send_to(src, dst.at[mine], n, device_of(k))

        dst[mine] = src[...]

    def wait_blocks(ref, number, sem):
        part = ref.at[pl.ds(0, number)]
        pltpu.make_async_copy(part, part, sem).wait()

    pl.semaphore_wait(barrier, owners - 1 + ring - 1)
    exchange(ask_ref, asked_ref, 0)
    asked_ref[me] = ask_ref[me]

    fetches[1].wait()
    for q in range(chunks):
        packed = lax.dot_general(
            place_ref[q * CHUNK : (q + 1) * CHUNK, :], cot_ref[...], NT, preferred_element_type=F32
        )
        block = slice(q * per, (q + 1) * per)
        send_ref[block, :, :width] = packed.reshape(per, cap, width).astype(BF16)
    send_ref[:, :, width:] = jnp.zeros((owners, cap, wide - width), BF16)
    back_ref[:, :, width:] = jnp.zeros((owners, cap, wide - width), BF16)
    exchange(send_ref, recv_ref, 1)
    recv_ref[me] = send_ref[me]

    fetches[2].wait()
    multiplier = 1.0 + weight_ref[...].reshape(1, width)
    fetches[3].wait()
    wait_blocks(asked_ref, owners - 1, recv_sems.at[0])

    lane = lax.broadcasted_iota(jnp.int32, (CHUNK, 128), 1)
    own_lane = lane == lax.rem(lax.broadcasted_iota(jnp.int32, (CHUNK, 128), 0), cap)
    entry = lax.broadcasted_iota(jnp.int32, (CHUNK, vrows), 1)

    def as_rows(columns):
        out = jnp.zeros((CHUNK, 128), F32)
        for q, column in enumerate(columns):
            out = jnp.where(lane == q, column, out)
        return out.T[:chunks, :]

    def as_columns(rows):
        filler = jnp.zeros((128 - chunks, 128), F32)
        return jnp.concatenate([rows, filler], axis=0).T

    sums = []
    for q in range(chunks):
        here = slice(q * CHUNK, (q + 1) * CHUNK)
        theirs = asked_ref[q * per : (q + 1) * per]
        theirs = jnp.broadcast_to(theirs, (per, cap, 128)).reshape(CHUNK, 128)
        number = jnp.sum(jnp.where(own_lane, theirs, 0), axis=1, keepdims=True)
        hot_ref[here, :] = jnp.where(number == entry, 1.0, 0.0).astype(BF16)
        rows = lax.dot_general(hot_ref[here, :], table_ref[...], NT, preferred_element_type=F32)
        unit_ref[here, :] = rows
        sums.append(jnp.sum(rows * rows, axis=1, keepdims=True))
    part_ref[0] = as_rows(sums)
    share(part_ref.at[0], square_ref, 2, col, ring, along)
    wait_blocks(square_ref, ring - 1, recv_sems.at[2])
    inverse = as_columns(lax.rsqrt(jnp.sum(square_ref[...], axis=0) + EPS))
    for q in range(chunks):
        here = slice(q * CHUNK, (q + 1) * CHUNK)
        unit = unit_ref[here, :] * scale * inverse[:, q : q + 1]
        unit_ref[here, :] = unit
        normed = (unit * multiplier).reshape(per, cap, width).astype(BF16)
        back_ref[q * per : (q + 1) * per, :, :width] = normed
    exchange(back_ref, done_ref, 3)
    done_ref[me] = back_ref[me]

    wait_blocks(recv_ref, owners - 1, recv_sems.at[1])

    def received(q):
        block = recv_ref[q * per : (q + 1) * per, :, :width].astype(F32)
        return block.reshape(CHUNK, width)

    sums = []
    total = jnp.zeros((1, width), F32)
    for q in range(chunks):
        here = slice(q * CHUNK, (q + 1) * CHUNK)
        product = received(q) * unit_ref[here, :]
        total += jnp.sum(product, axis=0, keepdims=True)
        sums.append(jnp.sum(product * multiplier, axis=1, keepdims=True))
    part_ref[1] = as_rows(sums)
    share(part_ref.at[1], inner_ref, 4, col, ring, along)
    wgp_ref[:, :width] = total
    wgp_ref[:, width:] = jnp.zeros((1, wide - width), F32)
    share(wgp_ref, wg1_ref, 5, inner_id, cores, beside)

    wait_blocks(inner_ref, ring - 1, recv_sems.at[4])
    inner = as_columns(jnp.sum(inner_ref[...], axis=0) * (1.0 / (width * ring)))
    for q in range(chunks):
        here = slice(q * CHUNK, (q + 1) * CHUNK)
        rest = received(q) * multiplier - unit_ref[here, :] * inner[:, q : q + 1]
        g_ref[here, :] = (scale * inverse[:, q : q + 1] * rest).astype(BF16)
    wait_blocks(wg1_ref, cores - 1, recv_sems.at[5])
    wgs_ref[...] = jnp.sum(wg1_ref[...], axis=0)
    share(wgs_ref, wg2_ref, 6, height, heights, above)

    grad_ref[...] = lax.dot_general(
        g_ref[...], hot_ref[...], TN, preferred_element_type=F32
    ).astype(BF16)

    wait_blocks(wg2_ref, heights - 1, recv_sems.at[6])
    wg_ref[...] = jnp.sum(wg2_ref[...], axis=0)[:, :width].reshape(width)
    wait_blocks(done_ref, owners - 1, recv_sems.at[3])
    arrived = done_ref[:, :, :width].astype(F32).reshape(slots, width).astype(BF16)
    normed_ref[...] = lax.dot_general(
        arrived, place_ref[...], TN, preferred_element_type=F32
    ).astype(BF16)

    for n, (ref, number) in enumerate(
        (
            (ask_ref, owners),
            (send_ref, owners),
            (square_ref, ring),
            (back_ref, owners),
            (inner_ref, ring),
            (wg1_ref, cores),
            (wg2_ref, heights),
        )
    ):
        wait_blocks(ref, number - 1, send_sems.at[n])


def body(mesh, token_ids, table, norm_weight, cotangent):
    groups, ring = mesh.shape["dp"], mesh.shape["mp"]
    owners = mesh.shape["section"] * groups
    vrows, width = table.shape
    count = token_ids.shape[0]
    cap = 2 * count // owners
    cores = 8
    heights = owners // cores
    slots = owners * cap
    chunks = slots // CHUNK
    wide = -(-width // 128) * 128
    operands = (token_ids.reshape(1, count), norm_weight, cotangent.T, table.T)
    vmem = pl.BlockSpec(memory_space=pltpu.VMEM)
    hbm = pl.BlockSpec(memory_space=pltpu.HBM)
    normed, weight_grad, table_grad = pl.pallas_call(
        functools.partial(kernel, (groups, ring, cap, cores)),
        out_shape=(
            jax.ShapeDtypeStruct((width, count), BF16),
            jax.ShapeDtypeStruct((width,), F32),
            jax.ShapeDtypeStruct((width, vrows), BF16),
        ),
        in_specs=[hbm, hbm, hbm, hbm],
        out_specs=(vmem, vmem, vmem),
        scratch_shapes=[
            pltpu.VMEM((1, count), jnp.int32),
            pltpu.VMEM((width,), F32),
            pltpu.VMEM((width, vrows), BF16),
            pltpu.VMEM((width, count), BF16),
            pltpu.VMEM((slots, count), BF16),
            pltpu.VMEM((owners, 1, 128), jnp.int32),
            pltpu.VMEM((owners, 1, 128), jnp.int32),
            pltpu.VMEM((owners, cap, wide), BF16),
            pltpu.VMEM((owners, cap, wide), BF16),
            pltpu.VMEM((slots, vrows), BF16),
            pltpu.VMEM((slots, width), F32),
            pltpu.VMEM((2, chunks, 128), F32),
            pltpu.VMEM((ring, chunks, 128), F32),
            pltpu.VMEM((ring, chunks, 128), F32),
            pltpu.VMEM((owners, cap, wide), BF16),
            pltpu.VMEM((owners, cap, wide), BF16),
            pltpu.VMEM((slots, width), BF16),
            pltpu.VMEM((1, wide), F32),
            pltpu.VMEM((cores, 1, wide), F32),
            pltpu.VMEM((1, wide), F32),
            pltpu.VMEM((heights, 1, wide), F32),
            pltpu.SemaphoreType.DMA((4,)),
            pltpu.SemaphoreType.DMA((7,)),
            pltpu.SemaphoreType.DMA((7,)),
        ],
        compiler_params=pltpu.CompilerParams(
            collective_id=0, has_side_effects=True, vmem_limit_bytes=32 * 1024 * 1024
        ),
    )(*(pltpu.with_memory_space_constraint(x, pltpu.HBM) for x in operands))
    return normed.T, weight_grad, table_grad.T


def solution(mesh):
    placed = (P(("section", "dp")), P(("section", "dp"), "mp"), P("mp"), P(("section", "dp"), "mp"))
    return jax.shard_map(
        functools.partial(body, mesh),
        mesh=mesh,
        in_specs=placed,
        out_specs=(P(("section", "dp"), "mp"), P("mp"), P(("section", "dp"), "mp")),
        check_vma=False,
    )
```

```python
import functools
import math

import jax
import jax.numpy as jnp
from jax import lax
from jax.experimental import pallas as pl
from jax.experimental.pallas import tpu as pltpu
from jax.sharding import PartitionSpec as P

MESH = pl.DeviceIdType.MESH
F32 = jnp.float32
BF16 = jnp.bfloat16
EPS = 1e-06
NT = (((1,), (1,)), ((), ()))
TN = (((0,), (0,)), ((), ()))

CHUNK = 128
STRIP = 64


def kernel(
    dims,
    ids_hbm,
    weight_hbm,
    cot_hbm,
    table_hbm,
    normed_ref,
    wg_ref,
    grad_ref,
    ids_ref,
    weight_ref,
    table_ref,
    cot_ref,
    place_ref,
    ask_ref,
    asked_ref,
    cot_out_refs,
    cot_in_refs,
    row_out_refs,
    row_in_refs,
    hot_ref,
    unit_ref,
    part_ref,
    square_ref,
    inner_ref,
    mult_ref,
    inv_ref,
    scaled_ref,
    square_part_ref,
    g_ref,
    wgp_ref,
    wg1_ref,
    wgs_ref,
    wg2_ref,
    local_sems,
    send_sems,
    recv_sems,
):
    groups, ring, cap, cores = dims
    owners = lax.axis_size("section") * groups
    heights = owners // cores
    width, count = cot_ref.shape
    vrows = table_ref.shape[1]
    slots = owners * cap
    wide = wgp_ref.shape[1]
    full = cot_out_refs[0].shape[2]
    rest = width - full
    scale = math.sqrt(width * ring)
    chunks = slots // CHUNK
    per = CHUNK // cap

    sec = lax.axis_index("section")
    grp = lax.axis_index("dp")
    col = lax.axis_index("mp")
    me = sec * groups + grp
    inner_id = lax.rem(sec, cores)
    height = lax.div(sec, cores) * groups + grp

    def plane(step):
        p = lax.rem(me + step, owners)
        return p, (lax.div(p, groups), lax.rem(p, groups), col)

    def along(step):
        return (sec, grp, lax.rem(col + step, ring))

    def beside(step):
        return (sec - inner_id + lax.rem(inner_id + step, cores), grp, col)

    def above(step):
        h = lax.rem(height + step, heights)
        return (lax.div(h, groups) * cores + inner_id, lax.rem(h, groups), col)

    barrier = pltpu.get_barrier_semaphore()

    @pl.loop(1, owners)
    def _(k):
        pl.semaphore_signal(barrier, inc=1, device_id=plane(k)[1], device_id_type=MESH)

    @pl.loop(1, ring)
    def _(k):
        pl.semaphore_signal(barrier, inc=1, device_id=along(k), device_id_type=MESH)

    fetches = [
        pltpu.make_async_copy(src, dst, local_sems.at[n])
        for n, (src, dst) in enumerate(
            (
                (ids_hbm, ids_ref),
                (cot_hbm, cot_ref),
                (weight_hbm, weight_ref),
                (table_hbm, table_ref.at[pl.ds(0, table_hbm.shape[0])]),
            )
        )
    ]
    for fetch in fetches:
        fetch.start()

    before = lax.broadcasted_iota(jnp.int32, (count, count), 0) < lax.broadcasted_iota(
        jnp.int32, (count, count), 1
    )
    before = jnp.where(before, 1.0, 0.0).astype(BF16)
    fetches[0].wait()
    ids = jnp.broadcast_to(ids_ref[...], (owners, count))
    local = ids - vrows * lax.broadcasted_iota(jnp.int32, (owners, count), 0)
    member = (local >= 0) & (local < vrows)
    rank = jnp.dot(
        jnp.where(member, 1.0, 0.0).astype(BF16), before, preferred_element_type=F32
    )
    rank = jnp.where(member, rank, -1.0)
    lane = lax.broadcasted_iota(jnp.int32, (owners, 128), 1)
    wanted = jnp.full((owners, 128), -1, jnp.int32)
    for s in range(cap):
        one = jnp.sum(jnp.where(rank == s, local + 1, 0), axis=1, keepdims=True) - 1
        wanted = jnp.where(lane == s, one, wanted)
    ask_ref[...] = wanted[:, None, :]
    slot_of = lax.broadcasted_iota(jnp.int32, (owners, cap, count), 1).astype(F32)
    place = jnp.where(rank[:, None, :] == slot_of, 1.0, 0.0).reshape(slots, count)
    place_ref[...] = place.astype(BF16)

    def send_to(src, dst, n, device):
        pltpu.make_async_remote_copy(
            src_ref=src,
            dst_ref=dst,
            send_sem=send_sems.at[n],
            recv_sem=recv_sems.at[n],
            device_id=device,
            device_id_type=MESH,
        ).start()

    def exchange(src, dst, n):
        @pl.loop(1, owners)
        def _(k):
            p, device = plane(k)
            for m, (one, other) in enumerate(zip(src, dst)):
                send_to(one.at[p], other.at[me], n + m, device)

        for one, other in zip(src, dst):
            other[me] = one[me]

    def share(src, dst, n, mine, number, device_of):
        @pl.loop(1, number)
        def _(k):
            send_to(src, dst.at[mine], n, device_of(k))

        dst[mine] = src[...]

    def wait_blocks(ref, number, sem):
        part = ref.at[pl.ds(0, number)]
        pltpu.make_async_copy(part, part, sem).wait()

    def put(refs, q, value):
        block = slice(q * per, (q + 1) * per)
        refs[0][block] = value[:, :full].reshape(per, cap, full).astype(BF16)
        last = value[:, full:].reshape(per, cap, rest)
        last = jnp.concatenate([last[:, : cap // 2], last[:, cap // 2 :]], axis=2)
        refs[1][block] = last.astype(BF16)

    def get(refs, q):
        block = slice(q * per, (q + 1) * per)
        last = refs[1][block].astype(F32)
        last = jnp.concatenate([last[:, :, :rest], last[:, :, rest:]], axis=1)
        first = refs[0][block].astype(F32).reshape(CHUNK, full)
        return jnp.concatenate([first, last.reshape(CHUNK, rest)], axis=1)

    pl.semaphore_wait(barrier, owners - 1 + ring - 1)
    exchange((ask_ref,), (asked_ref,), 0)

    fetches[3].wait()
    squares = jnp.zeros((1, vrows), F32)
    for first in range(0, width, STRIP):
        rows = table_ref[first : first + STRIP, :].astype(F32)
        squares += jnp.sum(rows * rows, axis=0, keepdims=True)
    square_part_ref[:, :vrows] = squares
    square_part_ref[:, vrows:] = jnp.zeros((1, square_part_ref.shape[1] - vrows), F32)
    share(square_part_ref, square_ref, 3, col, ring, along)

    fetches[1].wait()
    for q in range(chunks):
        packed = lax.dot_general(
            place_ref[q * CHUNK : (q + 1) * CHUNK, :], cot_ref[...], NT, preferred_element_type=F32
        )
        put(cot_out_refs, q, packed)
    exchange(cot_out_refs, cot_in_refs, 1)

    fetches[2].wait()
    multiplier = 1.0 + weight_ref[...].reshape(1, width)
    for first in range(0, width, 128):
        last = min(first + 128, width)
        row = jnp.broadcast_to(multiplier[:, first:last], (128, last - first))
        mult_ref[first:last, :] = row.T

    wait_blocks(square_ref, ring - 1, recv_sems.at[3])
    inverse = lax.rsqrt(jnp.sum(square_ref[...], axis=0)[:, :vrows] + EPS)
    for first in range(0, width, STRIP):
        strip = slice(first, first + STRIP)
        unit = table_ref[strip, :].astype(F32) * (scale * inverse)
        scaled_ref[strip, :] = (unit * mult_ref[strip, :1]).astype(BF16)
    high = inverse.astype(BF16).astype(F32)
    middle = (inverse - high).astype(BF16).astype(F32)
    low = inverse - high - middle
    line = lax.broadcasted_iota(jnp.int32, (16, vrows), 0)
    pieces = jnp.where(line == 0, high, jnp.where(line == 1, middle, jnp.where(line == 2, low, 0.0)))
    table_ref[width:, :] = pieces.astype(BF16)
    wait_blocks(asked_ref, owners - 1, recv_sems.at[0])

    lane = lax.broadcasted_iota(jnp.int32, (CHUNK, 128), 1)
    own_lane = lane == lax.rem(lax.broadcasted_iota(jnp.int32, (CHUNK, 128), 0), cap)
    entry = lax.broadcasted_iota(jnp.int32, (CHUNK, vrows), 1)

    def per_slot(ref, q, nothing):
        value = ref[q * per : (q + 1) * per]
        value = jnp.broadcast_to(value, (per, cap, 128)).reshape(CHUNK, 128)
        return jnp.sum(jnp.where(own_lane, value, nothing), axis=1, keepdims=True)

    def as_rows(columns):
        out = jnp.zeros((CHUNK, 128), F32)
        for q, column in enumerate(columns):
            out = jnp.where(lane == q, column, out)
        return out.T[:chunks, :]

    def as_columns(rows):
        filler = jnp.zeros((128 - chunks, 128), F32)
        return jnp.concatenate([rows, filler], axis=0).T

    for q in range(chunks):
        span = slice(q * CHUNK, (q + 1) * CHUNK)
        number = per_slot(asked_ref, q, 0)
        hot_ref[span, :] = jnp.where(number == entry, 1.0, 0.0).astype(BF16)
    normed = lax.dot_general(hot_ref[...], scaled_ref[...], NT, preferred_element_type=F32)
    for q in range(chunks):
        put(row_out_refs, q, normed[q * CHUNK : (q + 1) * CHUNK, :])
    exchange(row_out_refs, row_in_refs, 4)

    found = lax.dot_general(hot_ref[...], table_ref[...], NT, preferred_element_type=F32)
    inverse = (
        found[:, width : width + 1] + found[:, width + 1 : width + 2] + found[:, width + 2 : width + 3]
    )
    unit_ref[...] = found[:, :width] * (scale * inverse)
    inv_ref[...] = jnp.broadcast_to(inverse, (slots, 128))

    for n in range(2):
        wait_blocks(cot_in_refs[n], owners - 1, recv_sems.at[1 + n])
    sums = []
    total = jnp.zeros((1, width), F32)
    for q in range(chunks):
        span = slice(q * CHUNK, (q + 1) * CHUNK)
        product = get(cot_in_refs, q) * unit_ref[span, :]
        total += jnp.sum(product, axis=0, keepdims=True)
        sums.append(jnp.sum(product * multiplier, axis=1, keepdims=True))
    part_ref[...] = as_rows(sums)
    share(part_ref, inner_ref, 6, col, ring, along)
    wgp_ref[:, :width] = total
    wgp_ref[:, width:] = jnp.zeros((1, wide - width), F32)
    share(wgp_ref, wg1_ref, 7, inner_id, cores, beside)

    wait_blocks(wg1_ref, cores - 1, recv_sems.at[7])
    wgs_ref[...] = jnp.sum(wg1_ref[...], axis=0)
    share(wgs_ref, wg2_ref, 8, height, heights, above)
    wait_blocks(inner_ref, ring - 1, recv_sems.at[6])
    inner = as_columns(jnp.sum(inner_ref[...], axis=0) * (1.0 / (width * ring)))
    for q in range(chunks):
        span = slice(q * CHUNK, (q + 1) * CHUNK)
        left = get(cot_in_refs, q) * multiplier - unit_ref[span, :] * inner[:, q : q + 1]
        g_ref[span, :] = (scale * inv_ref[span, :1] * left).astype(BF16)

    grad_ref[...] = lax.dot_general(
        g_ref[...], hot_ref[...], TN, preferred_element_type=F32
    ).astype(BF16)

    wait_blocks(wg2_ref, heights - 1, recv_sems.at[8])
    wg_ref[...] = jnp.sum(wg2_ref[...], axis=0)[:, :width].reshape(width)
    for n in range(2):
        wait_blocks(row_in_refs[n], owners - 1, recv_sems.at[4 + n])
    arrived = [get(row_in_refs, q).astype(BF16) for q in range(chunks)]
    normed_ref[...] = lax.dot_general(
        jnp.concatenate(arrived, axis=0), place_ref[...], TN, preferred_element_type=F32
    ).astype(BF16)

    for n, (ref, number) in enumerate(
        (
            (ask_ref, owners),
            (cot_out_refs[0], owners),
            (cot_out_refs[1], owners),
            (square_ref, ring),
            (row_out_refs[0], owners),
            (row_out_refs[1], owners),
            (inner_ref, ring),
            (wg1_ref, cores),
            (wg2_ref, heights),
        )
    ):
        wait_blocks(ref, number - 1, send_sems.at[n])


def body(mesh, token_ids, table, norm_weight, cotangent):
    groups, ring = mesh.shape["dp"], mesh.shape["mp"]
    owners = mesh.shape["section"] * groups
    vrows, width = table.shape
    count = token_ids.shape[0]
    cap = 2 * count // owners
    cores = 8
    heights = owners // cores
    slots = owners * cap
    chunks = slots // CHUNK
    wide = -(-width // 128) * 128
    operands = (token_ids.reshape(1, count), norm_weight, cotangent.T, table.T)
    full = width // 128 * 128
    blocks = (
        pltpu.VMEM((owners, cap, full), BF16),
        pltpu.VMEM((owners, cap // 2, 2 * (width - full)), BF16),
    )
    vmem = pl.BlockSpec(memory_space=pltpu.VMEM)
    hbm = pl.BlockSpec(memory_space=pltpu.HBM)
    normed, weight_grad, table_grad = pl.pallas_call(
        functools.partial(kernel, (groups, ring, cap, cores)),
        out_shape=(
            jax.ShapeDtypeStruct((width, count), BF16),
            jax.ShapeDtypeStruct((width,), F32),
            jax.ShapeDtypeStruct((width, vrows), BF16),
        ),
        in_specs=[hbm, hbm, hbm, hbm],
        out_specs=(vmem, vmem, vmem),
        scratch_shapes=[
            pltpu.VMEM((1, count), jnp.int32),
            pltpu.VMEM((width,), F32),
            pltpu.VMEM((width + 16, vrows), BF16),
            pltpu.VMEM((width, count), BF16),
            pltpu.VMEM((slots, count), BF16),
            pltpu.VMEM((owners, 1, 128), jnp.int32),
            pltpu.VMEM((owners, 1, 128), jnp.int32),
            blocks,
            blocks,
            blocks,
            blocks,
            pltpu.VMEM((slots, vrows), BF16),
            pltpu.VMEM((slots, width), F32),
            pltpu.VMEM((chunks, 128), F32),
            pltpu.VMEM((ring, 1, -(-vrows // 128) * 128), F32),
            pltpu.VMEM((ring, chunks, 128), F32),
            pltpu.VMEM((width, 128), F32),
            pltpu.VMEM((slots, 128), F32),
            pltpu.VMEM((width, vrows), BF16),
            pltpu.VMEM((1, -(-vrows // 128) * 128), F32),
            pltpu.VMEM((slots, width), BF16),
            pltpu.VMEM((1, wide), F32),
            pltpu.VMEM((cores, 1, wide), F32),
            pltpu.VMEM((1, wide), F32),
            pltpu.VMEM((heights, 1, wide), F32),
            pltpu.SemaphoreType.DMA((4,)),
            pltpu.SemaphoreType.DMA((9,)),
            pltpu.SemaphoreType.DMA((9,)),
        ],
        compiler_params=pltpu.CompilerParams(
            collective_id=0, has_side_effects=True, vmem_limit_bytes=32 * 1024 * 1024
        ),
    )(*(pltpu.with_memory_space_constraint(x, pltpu.HBM) for x in operands))
    return normed.T, weight_grad, table_grad.T


def solution(mesh):
    placed = (P(("section", "dp")), P(("section", "dp"), "mp"), P("mp"), P(("section", "dp"), "mp"))
    return jax.shard_map(
        functools.partial(body, mesh),
        mesh=mesh,
        in_specs=placed,
        out_specs=(P(("section", "dp"), "mp"), P("mp"), P(("section", "dp"), "mp")),
        check_vma=False,
    )
```

```python
import functools
import math

import jax
import jax.numpy as jnp
from jax import lax
from jax.experimental import pallas as pl
from jax.experimental.pallas import tpu as pltpu
from jax.sharding import PartitionSpec as P

MESH = pl.DeviceIdType.MESH
F32 = jnp.float32
BF16 = jnp.bfloat16
EPS = 1e-06
NT = (((1,), (1,)), ((), ()))
TN = (((0,), (0,)), ((), ()))

CHUNK = 128
STRIP = 64


def get(refs, q):
    cap, full = refs[0].shape[1:]
    rest = refs[1].shape[2] // 2
    block = slice(q * CHUNK // cap, (q + 1) * CHUNK // cap)
    last = refs[1][block].astype(F32)
    last = jnp.concatenate([last[:, :, :rest], last[:, :, rest:]], axis=1)
    first = refs[0][block].astype(F32).reshape(CHUNK, full)
    return jnp.concatenate([first, last.reshape(CHUNK, rest)], axis=1)


def finish(
    first_ref,
    last_ref,
    place_ref,
    total_ref,
    grad_ref,
    normed_hbm,
    wg_hbm,
    grad_hbm,
    normed_ref,
    wg_ref,
    sems,
):
    grad_copy = pltpu.make_async_copy(grad_ref, grad_hbm, sems.at[0])
    grad_copy.start()
    wg_ref[...] = total_ref[...].reshape(total_ref.shape[1])[: wg_ref.shape[0]]
    wg_copy = pltpu.make_async_copy(wg_ref, wg_hbm, sems.at[1])
    wg_copy.start()
    refs = (first_ref, last_ref)
    arrived = [get(refs, q).astype(BF16) for q in range(place_ref.shape[0] // CHUNK)]
    normed_ref[...] = lax.dot_general(
        jnp.concatenate(arrived, axis=0), place_ref[...], TN, preferred_element_type=F32
    ).astype(BF16)
    normed_copy = pltpu.make_async_copy(normed_ref, normed_hbm, sems.at[2])
    normed_copy.start()
    grad_copy.wait()
    wg_copy.wait()
    normed_copy.wait()


def kernel(
    dims,
    ids_hbm,
    weight_hbm,
    cot_hbm,
    table_hbm,
    row_first_ref,
    row_last_ref,
    place_ref,
    wg_ref,
    grad_ref,
    ids_ref,
    weight_ref,
    table_ref,
    cot_ref,
    ask_ref,
    asked_ref,
    cot_out_refs,
    cot_in_refs,
    row_out_refs,
    hot_ref,
    unit_ref,
    part_ref,
    square_ref,
    inner_ref,
    mult_ref,
    inv_ref,
    scaled_ref,
    square_part_ref,
    g_ref,
    wgp_ref,
    wg1_ref,
    wgs_ref,
    wg2_ref,
    local_sems,
    send_sems,
    recv_sems,
):
    groups, ring, cap, cores = dims
    owners = lax.axis_size("section") * groups
    heights = owners // cores
    width, count = cot_ref.shape
    vrows = table_ref.shape[1]
    slots = owners * cap
    wide = wgp_ref.shape[1]
    full = cot_out_refs[0].shape[2]
    rest = width - full
    scale = math.sqrt(width * ring)
    chunks = slots // CHUNK
    per = CHUNK // cap

    sec = lax.axis_index("section")
    grp = lax.axis_index("dp")
    col = lax.axis_index("mp")
    me = sec * groups + grp
    inner_id = lax.rem(sec, cores)
    height = lax.div(sec, cores) * groups + grp

    def plane(step):
        p = lax.rem(me + step, owners)
        return p, (lax.div(p, groups), lax.rem(p, groups), col)

    def along(step):
        return (sec, grp, lax.rem(col + step, ring))

    def beside(step):
        return (sec - inner_id + lax.rem(inner_id + step, cores), grp, col)

    def above(step):
        h = lax.rem(height + step, heights)
        return (lax.div(h, groups) * cores + inner_id, lax.rem(h, groups), col)

    row_in_refs = (row_first_ref, row_last_ref)
    barrier = pltpu.get_barrier_semaphore()

    @pl.loop(1, owners, unroll=7)
    def _(k):
        pl.semaphore_signal(barrier, inc=1, device_id=plane(k)[1], device_id_type=MESH)

    @pl.loop(1, ring)
    def _(k):
        pl.semaphore_signal(barrier, inc=1, device_id=along(k), device_id_type=MESH)

    fetches = [
        pltpu.make_async_copy(src, dst, local_sems.at[n])
        for n, (src, dst) in enumerate(
            (
                (ids_hbm, ids_ref),
                (cot_hbm, cot_ref),
                (weight_hbm, weight_ref),
                (table_hbm, table_ref.at[pl.ds(0, table_hbm.shape[0])]),
            )
        )
    ]
    for fetch in fetches:
        fetch.start()

    before = lax.broadcasted_iota(jnp.int32, (count, count), 0) < lax.broadcasted_iota(
        jnp.int32, (count, count), 1
    )
    before = jnp.where(before, 1.0, 0.0).astype(BF16)
    fetches[0].wait()
    ids = jnp.broadcast_to(ids_ref[...], (owners, count))
    local = ids - vrows * lax.broadcasted_iota(jnp.int32, (owners, count), 0)
    member = (local >= 0) & (local < vrows)
    rank = jnp.dot(
        jnp.where(member, 1.0, 0.0).astype(BF16), before, preferred_element_type=F32
    )
    rank = jnp.where(member, rank, -1.0)
    lane = lax.broadcasted_iota(jnp.int32, (owners, 128), 1)
    wanted = jnp.full((owners, 128), -1, jnp.int32)
    for s in range(cap):
        one = jnp.sum(jnp.where(rank == s, local + 1, 0), axis=1, keepdims=True) - 1
        wanted = jnp.where(lane == s, one, wanted)
    ask_ref[...] = wanted[:, None, :]
    slot_of = lax.broadcasted_iota(jnp.int32, (owners, cap, count), 1).astype(F32)
    place = jnp.where(rank[:, None, :] == slot_of, 1.0, 0.0).reshape(slots, count)
    place_ref[...] = place.astype(BF16)

    def send_to(src, dst, n, device):
        pltpu.make_async_remote_copy(
            src_ref=src,
            dst_ref=dst,
            send_sem=send_sems.at[n],
            recv_sem=recv_sems.at[n],
            device_id=device,
            device_id_type=MESH,
        ).start()

    def exchange(src, dst, n):
        @pl.loop(1, owners, unroll=7)
        def _(k):
            p, device = plane(k)
            for m, (one, other) in enumerate(zip(src, dst)):
                send_to(one.at[p], other.at[me], n + m, device)

        for one, other in zip(src, dst):
            other[me] = one[me]

    def share(src, dst, n, mine, number, device_of):
        @pl.loop(1, number)
        def _(k):
            send_to(src, dst.at[mine], n, device_of(k))

        dst[mine] = src[...]

    def wait_blocks(ref, number, sem):
        part = ref.at[pl.ds(0, number)]
        pltpu.make_async_copy(part, part, sem).wait()

    def put(refs, q, value):
        block = slice(q * per, (q + 1) * per)
        refs[0][block] = value[:, :full].reshape(per, cap, full).astype(BF16)
        last = value[:, full:].reshape(per, cap, rest)
        last = jnp.concatenate([last[:, : cap // 2], last[:, cap // 2 :]], axis=2)
        refs[1][block] = last.astype(BF16)

    fetches[1].wait()
    for q in range(chunks):
        packed = lax.dot_general(
            place_ref[q * CHUNK : (q + 1) * CHUNK, :], cot_ref[...], NT, preferred_element_type=F32
        )
        put(cot_out_refs, q, packed)
    fetches[3].wait()
    squares = jnp.zeros((1, vrows), F32)
    for first in range(0, width, STRIP):
        rows = table_ref[first : first + STRIP, :].astype(F32)
        squares += jnp.sum(rows * rows, axis=0, keepdims=True)
    square_part_ref[:, :vrows] = squares
    square_part_ref[:, vrows:] = jnp.zeros((1, square_part_ref.shape[1] - vrows), F32)
    pl.semaphore_wait(barrier, owners - 1 + ring - 1)
    exchange((ask_ref,), (asked_ref,), 0)

    share(square_part_ref, square_ref, 3, col, ring, along)

    exchange(cot_out_refs, cot_in_refs, 1)

    fetches[2].wait()
    multiplier = 1.0 + weight_ref[...].reshape(1, width)
    for first in range(0, width, 128):
        last = min(first + 128, width)
        row = jnp.broadcast_to(multiplier[:, first:last], (128, last - first))
        mult_ref[first:last, :] = row.T

    wait_blocks(square_ref, ring - 1, recv_sems.at[3])
    inverse = lax.rsqrt(jnp.sum(square_ref[...], axis=0)[:, :vrows] + EPS)
    for first in range(0, width, STRIP):
        strip = slice(first, first + STRIP)
        unit = table_ref[strip, :].astype(F32) * (scale * inverse)
        scaled_ref[strip, :] = (unit * mult_ref[strip, :1]).astype(BF16)
    high = inverse.astype(BF16).astype(F32)
    middle = (inverse - high).astype(BF16).astype(F32)
    low = inverse - high - middle
    line = lax.broadcasted_iota(jnp.int32, (16, vrows), 0)
    pieces = jnp.where(line == 0, high, jnp.where(line == 1, middle, jnp.where(line == 2, low, 0.0)))
    table_ref[width:, :] = pieces.astype(BF16)
    wait_blocks(asked_ref, owners - 1, recv_sems.at[0])

    lane = lax.broadcasted_iota(jnp.int32, (CHUNK, 128), 1)
    own_lane = lane == lax.rem(lax.broadcasted_iota(jnp.int32, (CHUNK, 128), 0), cap)
    entry = lax.broadcasted_iota(jnp.int32, (CHUNK, vrows), 1)

    def per_slot(ref, q, nothing):
        value = ref[q * per : (q + 1) * per]
        value = jnp.broadcast_to(value, (per, cap, 128)).reshape(CHUNK, 128)
        return jnp.sum(jnp.where(own_lane, value, nothing), axis=1, keepdims=True)

    def as_rows(columns):
        out = jnp.zeros((CHUNK, 128), F32)
        for q, column in enumerate(columns):
            out = jnp.where(lane == q, column, out)
        return out.T[:chunks, :]

    def as_columns(rows):
        filler = jnp.zeros((128 - chunks, 128), F32)
        return jnp.concatenate([rows, filler], axis=0).T

    for q in range(chunks):
        span = slice(q * CHUNK, (q + 1) * CHUNK)
        number = per_slot(asked_ref, q, 0)
        hot_ref[span, :] = jnp.where(number == entry, 1.0, 0.0).astype(BF16)
    normed = lax.dot_general(hot_ref[...], scaled_ref[...], NT, preferred_element_type=F32)
    for q in range(chunks):
        put(row_out_refs, q, normed[q * CHUNK : (q + 1) * CHUNK, :])
    exchange(row_out_refs, row_in_refs, 4)

    found = lax.dot_general(hot_ref[...], table_ref[...], NT, preferred_element_type=F32)
    inverse = (
        found[:, width : width + 1] + found[:, width + 1 : width + 2] + found[:, width + 2 : width + 3]
    )
    unit_ref[...] = found[:, :width] * (scale * inverse)
    inv_ref[...] = jnp.broadcast_to(inverse, (slots, 128))

    for n in range(2):
        wait_blocks(cot_in_refs[n], owners - 1, recv_sems.at[1 + n])
    sums = []
    total = jnp.zeros((1, width), F32)
    for q in range(chunks):
        span = slice(q * CHUNK, (q + 1) * CHUNK)
        product = get(cot_in_refs, q) * unit_ref[span, :]
        total += jnp.sum(product, axis=0, keepdims=True)
        sums.append(jnp.sum(product * multiplier, axis=1, keepdims=True))
    part_ref[...] = as_rows(sums)
    share(part_ref, inner_ref, 6, col, ring, along)
    wgp_ref[:, :width] = total
    wgp_ref[:, width:] = jnp.zeros((1, wide - width), F32)
    share(wgp_ref, wg1_ref, 7, inner_id, cores, beside)

    wait_blocks(wg1_ref, cores - 1, recv_sems.at[7])
    wgs_ref[...] = jnp.sum(wg1_ref[...], axis=0)
    share(wgs_ref, wg2_ref, 8, height, heights, above)
    wait_blocks(inner_ref, ring - 1, recv_sems.at[6])
    inner = as_columns(jnp.sum(inner_ref[...], axis=0) * (1.0 / (width * ring)))
    for q in range(chunks):
        span = slice(q * CHUNK, (q + 1) * CHUNK)
        left = get(cot_in_refs, q) * multiplier - unit_ref[span, :] * inner[:, q : q + 1]
        g_ref[span, :] = (scale * inv_ref[span, :1] * left).astype(BF16)

    grad_ref[...] = lax.dot_general(
        g_ref[...], hot_ref[...], TN, preferred_element_type=F32
    ).astype(BF16)

    wait_blocks(wg2_ref, heights - 1, recv_sems.at[8])
    wg_ref[...] = jnp.sum(wg2_ref[...], axis=0)
    for n in range(2):
        wait_blocks(row_in_refs[n], owners - 1, recv_sems.at[4 + n])
    for n, (ref, number) in enumerate(
        (
            (ask_ref, owners),
            (cot_out_refs[0], owners),
            (cot_out_refs[1], owners),
            (square_ref, ring),
            (row_out_refs[0], owners),
            (row_out_refs[1], owners),
            (inner_ref, ring),
            (wg1_ref, cores),
            (wg2_ref, heights),
        )
    ):
        wait_blocks(ref, number - 1, send_sems.at[n])


def body(mesh, token_ids, table, norm_weight, cotangent):
    groups, ring = mesh.shape["dp"], mesh.shape["mp"]
    owners = mesh.shape["section"] * groups
    vrows, width = table.shape
    count = token_ids.shape[0]
    cap = 2 * count // owners
    cores = 8
    heights = owners // cores
    slots = owners * cap
    chunks = slots // CHUNK
    wide = -(-width // 128) * 128
    operands = (token_ids.reshape(1, count), norm_weight, cotangent.T, table.T)
    full = width // 128 * 128
    blocks = (
        pltpu.VMEM((owners, cap, full), BF16),
        pltpu.VMEM((owners, cap // 2, 2 * (width - full)), BF16),
    )
    vmem = pl.BlockSpec(memory_space=pltpu.VMEM)
    hbm = pl.BlockSpec(memory_space=pltpu.HBM)
    block_shapes = tuple(jax.ShapeDtypeStruct(block.shape, BF16) for block in blocks)
    parts = pl.pallas_call(
        functools.partial(kernel, (groups, ring, cap, cores)),
        out_shape=(
            *block_shapes,
            jax.ShapeDtypeStruct((slots, count), BF16),
            jax.ShapeDtypeStruct((1, wide), F32),
            jax.ShapeDtypeStruct((width, vrows), BF16),
        ),
        in_specs=[hbm] * 4,
        out_specs=(vmem,) * 5,
        scratch_shapes=[
            pltpu.VMEM((1, count), jnp.int32),
            pltpu.VMEM((width,), F32),
            pltpu.VMEM((width + 16, vrows), BF16),
            pltpu.VMEM((width, count), BF16),
            pltpu.VMEM((owners, 1, 128), jnp.int32),
            pltpu.VMEM((owners, 1, 128), jnp.int32),
            blocks,
            blocks,
            blocks,
            pltpu.VMEM((slots, vrows), BF16),
            pltpu.VMEM((slots, width), F32),
            pltpu.VMEM((chunks, 128), F32),
            pltpu.VMEM((ring, 1, -(-vrows // 128) * 128), F32),
            pltpu.VMEM((ring, chunks, 128), F32),
            pltpu.VMEM((width, 128), F32),
            pltpu.VMEM((slots, 128), F32),
            pltpu.VMEM((width, vrows), BF16),
            pltpu.VMEM((1, -(-vrows // 128) * 128), F32),
            pltpu.VMEM((slots, width), BF16),
            pltpu.VMEM((1, wide), F32),
            pltpu.VMEM((cores, 1, wide), F32),
            pltpu.VMEM((1, wide), F32),
            pltpu.VMEM((heights, 1, wide), F32),
            pltpu.SemaphoreType.DMA((4,)),
            pltpu.SemaphoreType.DMA((9,)),
            pltpu.SemaphoreType.DMA((9,)),
        ],
        compiler_params=pltpu.CompilerParams(
            collective_id=0, has_side_effects=True, vmem_limit_bytes=32 * 1024 * 1024
        ),
    )(*(pltpu.with_memory_space_constraint(x, pltpu.HBM) for x in operands))
    normed, weight_grad, table_grad = pl.pallas_call(
        finish,
        out_shape=(
            jax.ShapeDtypeStruct((width, count), BF16),
            jax.ShapeDtypeStruct((width,), F32),
            jax.ShapeDtypeStruct((width, vrows), BF16),
        ),
        in_specs=[vmem] * 5,
        out_specs=(hbm,) * 3,
        scratch_shapes=[
            pltpu.VMEM((width, count), BF16),
            pltpu.VMEM((width,), F32),
            pltpu.SemaphoreType.DMA((3,)),
        ],
        compiler_params=pltpu.CompilerParams(vmem_limit_bytes=32 * 1024 * 1024),
    )(*parts)
    return normed.T, weight_grad, table_grad.T


def solution(mesh):
    placed = (P(("section", "dp")), P(("section", "dp"), "mp"), P("mp"), P(("section", "dp"), "mp"))
    return jax.shard_map(
        functools.partial(body, mesh),
        mesh=mesh,
        in_specs=placed,
        out_specs=(P(("section", "dp"), "mp"), P("mp"), P(("section", "dp"), "mp")),
        check_vma=False,
    )
```

```python
import functools
import math

import jax
import jax.numpy as jnp
from jax import lax
from jax.experimental import pallas as pl
from jax.experimental.pallas import tpu as pltpu
from jax.sharding import PartitionSpec as P

MESH = pl.DeviceIdType.MESH
F32 = jnp.float32
BF16 = jnp.bfloat16
EPS = 1e-06
NT = (((1,), (1,)), ((), ()))
TN = (((0,), (0,)), ((), ()))

CHUNK = 128
BEHIND = 43
STRIP = 64


def get(refs, q):
    cap, full = refs[0].shape[1:]
    rest = refs[1].shape[2] // 2
    block = slice(q * CHUNK // cap, (q + 1) * CHUNK // cap)
    last = refs[1][block].astype(F32)
    last = jnp.concatenate([last[:, :, :rest], last[:, :, rest:]], axis=1)
    first = refs[0][block].astype(F32).reshape(CHUNK, full)
    return jnp.concatenate([first, last.reshape(CHUNK, rest)], axis=1)


def finish(
    first_ref,
    last_ref,
    place_ref,
    total_ref,
    grad_ref,
    normed_hbm,
    wg_hbm,
    grad_hbm,
    normed_ref,
    wg_ref,
    sems,
):
    grad_copy = pltpu.make_async_copy(grad_ref, grad_hbm, sems.at[0])
    grad_copy.start()
    wg_ref[...] = total_ref[...].reshape(total_ref.shape[1])[: wg_ref.shape[0]]
    wg_copy = pltpu.make_async_copy(wg_ref, wg_hbm, sems.at[1])
    wg_copy.start()
    refs = (first_ref, last_ref)
    arrived = [get(refs, q).astype(BF16) for q in range(place_ref.shape[0] // CHUNK)]
    normed_ref[...] = lax.dot_general(
        jnp.concatenate(arrived, axis=0), place_ref[...], TN, preferred_element_type=F32
    ).astype(BF16)
    normed_copy = pltpu.make_async_copy(normed_ref, normed_hbm, sems.at[2])
    normed_copy.start()
    grad_copy.wait()
    wg_copy.wait()
    normed_copy.wait()


def kernel(
    dims,
    ids_hbm,
    weight_hbm,
    cot_hbm,
    table_hbm,
    row_first_ref,
    row_last_ref,
    place_ref,
    wg_ref,
    grad_ref,
    ids_ref,
    weight_ref,
    table_ref,
    cot_ref,
    ask_ref,
    asked_ref,
    cot_out_refs,
    cot_in_refs,
    row_out_refs,
    hot_ref,
    unit_ref,
    part_ref,
    square_ref,
    square_sum_ref,
    square_other_ref,
    inner_ref,
    inner_sum_ref,
    inner_other_ref,
    mult_ref,
    inv_ref,
    scaled_ref,
    square_part_ref,
    g_ref,
    wgp_ref,
    wg1_ref,
    wgs_ref,
    wg2_ref,
    local_sems,
    send_sems,
    recv_sems,
):
    groups, ring, cap, cores = dims
    owners = lax.axis_size("section") * groups
    heights = owners // cores
    width, count = cot_ref.shape
    vrows = table_ref.shape[1]
    slots = owners * cap
    wide = wgp_ref.shape[1]
    full = cot_out_refs[0].shape[2]
    rest = width - full
    scale = math.sqrt(width * ring)
    chunks = slots // CHUNK
    per = CHUNK // cap

    sec = lax.axis_index("section")
    grp = lax.axis_index("dp")
    col = lax.axis_index("mp")
    me = sec * groups + grp
    inner_id = lax.rem(sec, cores)
    height = lax.div(sec, cores) * groups + grp

    def plane(step):
        p = lax.rem(me + step, owners)
        return p, (lax.div(p, groups), lax.rem(p, groups), col)

    half = ring // 2
    place_in_half = lax.rem(col, half)
    downward = ((ring - 1, (0, 1)), (half, (half - 1, half - 2)))
    upward = (half - 1, half)

    def at(c):
        return (sec, grp, c)

    def along(step):
        return at(col - place_in_half + lax.rem(place_in_half + step, half))

    def beside(step):
        return (sec - inner_id + lax.rem(inner_id + step, cores), grp, col)

    def above(step):
        h = lax.rem(height + step, heights)
        return (lax.div(h, groups) * cores + inner_id, lax.rem(h, groups), col)

    row_in_refs = (row_first_ref, row_last_ref)
    barrier = pltpu.get_barrier_semaphore()

    @pl.loop(1, owners, unroll=7)
    def _(k):
        pl.semaphore_signal(barrier, inc=1, device_id=plane(k)[1], device_id_type=MESH)

    def greet(device):
        pl.semaphore_signal(barrier, inc=1, device_id=device, device_id_type=MESH)

    @pl.loop(1, half)
    def _(k):
        greet(along(k))

    for sender, receivers in (*downward, (upward[0], (upward[1],))):
        for receiver in receivers:

            @pl.when(col == receiver)
            def _():
                greet(at(sender))

    fetches = [
        pltpu.make_async_copy(src, dst, local_sems.at[n])
        for n, (src, dst) in enumerate(
            (
                (ids_hbm, ids_ref),
                (cot_hbm, cot_ref),
                (weight_hbm, weight_ref),
                (table_hbm, table_ref.at[pl.ds(0, table_hbm.shape[0])]),
            )
        )
    ]
    for fetch in fetches:
        fetch.start()

    before = lax.broadcasted_iota(jnp.int32, (count, count), 0) < lax.broadcasted_iota(
        jnp.int32, (count, count), 1
    )
    before = jnp.where(before, 1.0, 0.0).astype(BF16)
    fetches[0].wait()
    ids = jnp.broadcast_to(ids_ref[...], (owners, count))
    local = ids - vrows * lax.broadcasted_iota(jnp.int32, (owners, count), 0)
    member = (local >= 0) & (local < vrows)
    rank = jnp.dot(
        jnp.where(member, 1.0, 0.0).astype(BF16), before, preferred_element_type=F32
    )
    rank = jnp.where(member, rank, -1.0)
    lane = lax.broadcasted_iota(jnp.int32, (owners, 128), 1)
    wanted = jnp.full((owners, 128), -1, jnp.int32)
    for s in range(cap):
        one = jnp.sum(jnp.where(rank == s, local + 1, 0), axis=1, keepdims=True) - 1
        wanted = jnp.where(lane == s, one, wanted)
    ask_ref[...] = wanted[:, None, :]
    slot_of = lax.broadcasted_iota(jnp.int32, (owners, cap, count), 1).astype(F32)
    place = jnp.where(rank[:, None, :] == slot_of, 1.0, 0.0).reshape(slots, count)
    place_ref[...] = place.astype(BF16)

    def send_to(src, dst, n, device, sent=None):
        pltpu.make_async_remote_copy(
            src_ref=src,
            dst_ref=dst,
            send_sem=send_sems.at[n if sent is None else sent],
            recv_sem=recv_sems.at[n],
            device_id=device,
            device_id_type=MESH,
        ).start()

    def exchange(src, dst, n, first=1, last=owners):
        @pl.loop(first, last, unroll=7)
        def _(k):
            p, device = plane(k)
            for m, (one, other) in enumerate(zip(src, dst)):
                send_to(one.at[p], other.at[me], n + m, device)

        if first == 1:
            for one, other in zip(src, dst):
                other[me] = one[me]

    def share(src, dst, n, mine, number, device_of):
        @pl.loop(1, number)
        def _(k):
            send_to(src, dst.at[mine], n, device_of(k))

        dst[mine] = src[...]

    def wait_blocks(ref, number, sem):
        part = ref.at[pl.ds(0, number)]
        pltpu.make_async_copy(part, part, sem).wait()

    def start_sum(src, gathered, n):
        share(src, gathered, n, place_in_half, half, along)

    def cross(gathered, summed, other, n, meanwhile=None):
        wait_blocks(gathered, half - 1, recv_sems.at[n])
        summed[0] = jnp.sum(gathered[...], axis=0)
        for sender, receivers in (*downward, (upward[0], (upward[1],))):

            @pl.when(col == sender)
            def _():
                for receiver in receivers:
                    send_to(summed.at[0], other.at[0], n + 1, at(receiver))

        if meanwhile is not None:
            meanwhile()
        wait_blocks(other, 1, recv_sems.at[n + 1])

        @pl.when(col == upward[1])
        def _():
            for receiver in range(half + 1, ring):
                send_to(other.at[0], other.at[0], n + 1, at(receiver), n + 2)

        return summed[0] + other[0]

    def end_sum(gathered, n):
        wait_blocks(gathered, half - 1, send_sems.at[n])
        for sender, receivers in (*downward, (upward[0], (upward[1],))):

            @pl.when(col == sender)
            def _():
                wait_blocks(gathered, len(receivers), send_sems.at[n + 1])

        @pl.when(col == upward[1])
        def _():
            wait_blocks(gathered, half - 1, send_sems.at[n + 2])

    def put(refs, q, value):
        block = slice(q * per, (q + 1) * per)
        refs[0][block] = value[:, :full].reshape(per, cap, full).astype(BF16)
        last = value[:, full:].reshape(per, cap, rest)
        last = jnp.concatenate([last[:, : cap // 2], last[:, cap // 2 :]], axis=2)
        refs[1][block] = last.astype(BF16)

    fetches[1].wait()
    for q in range(chunks):
        packed = lax.dot_general(
            place_ref[q * CHUNK : (q + 1) * CHUNK, :], cot_ref[...], NT, preferred_element_type=F32
        )
        put(cot_out_refs, q, packed)
    fetches[3].wait()
    squares = jnp.zeros((1, vrows), F32)
    for first in range(0, width, STRIP):
        rows = table_ref[first : first + STRIP, :].astype(F32)
        squares += jnp.sum(rows * rows, axis=0, keepdims=True)
    square_part_ref[:, :vrows] = squares
    square_part_ref[:, vrows:] = jnp.zeros((1, square_part_ref.shape[1] - vrows), F32)
    crossing = (*downward, (upward[0], (upward[1],)))
    for sender, receivers in crossing:

        @pl.when(col == sender)
        def _():
            pl.semaphore_wait(barrier, owners - 1 + half - 1 + len(receivers))

    @pl.when((col != crossing[0][0]) & (col != crossing[1][0]) & (col != crossing[2][0]))
    def _():
        pl.semaphore_wait(barrier, owners - 1 + half - 1)

    exchange((ask_ref,), (asked_ref,), 0)

    start_sum(square_part_ref, square_ref, 7)

    exchange(cot_out_refs, cot_in_refs, 1)

    fetches[2].wait()
    multiplier = 1.0 + weight_ref[...].reshape(1, width)
    for first in range(0, width, 128):
        last = min(first + 128, width)
        row = jnp.broadcast_to(multiplier[:, first:last], (128, last - first))
        mult_ref[first:last, :] = row.T

    squares = cross(square_ref, square_sum_ref, square_other_ref, 7)
    inverse = lax.rsqrt(squares[:, :vrows] + EPS)
    for first in range(0, width, STRIP):
        strip = slice(first, first + STRIP)
        unit = table_ref[strip, :].astype(F32) * (scale * inverse)
        scaled_ref[strip, :] = (unit * mult_ref[strip, :1]).astype(BF16)
    high = inverse.astype(BF16).astype(F32)
    middle = (inverse - high).astype(BF16).astype(F32)
    low = inverse - high - middle
    line = lax.broadcasted_iota(jnp.int32, (16, vrows), 0)
    pieces = jnp.where(line == 0, high, jnp.where(line == 1, middle, jnp.where(line == 2, low, 0.0)))
    table_ref[width:, :] = pieces.astype(BF16)
    wait_blocks(asked_ref, owners - 1, recv_sems.at[0])

    lane = lax.broadcasted_iota(jnp.int32, (CHUNK, 128), 1)
    own_lane = lane == lax.rem(lax.broadcasted_iota(jnp.int32, (CHUNK, 128), 0), cap)
    entry = lax.broadcasted_iota(jnp.int32, (CHUNK, vrows), 1)

    def per_slot(ref, q, nothing):
        value = ref[q * per : (q + 1) * per]
        value = jnp.broadcast_to(value, (per, cap, 128)).reshape(CHUNK, 128)
        return jnp.sum(jnp.where(own_lane, value, nothing), axis=1, keepdims=True)

    def as_rows(columns):
        out = jnp.zeros((CHUNK, 128), F32)
        for q, column in enumerate(columns):
            out = jnp.where(lane == q, column, out)
        return out.T[:chunks, :]

    def as_columns(rows):
        filler = jnp.zeros((128 - chunks, 128), F32)
        return jnp.concatenate([rows, filler], axis=0).T

    for q in range(chunks):
        span = slice(q * CHUNK, (q + 1) * CHUNK)
        number = per_slot(asked_ref, q, 0)
        hot_ref[span, :] = jnp.where(number == entry, 1.0, 0.0).astype(BF16)
    normed = lax.dot_general(hot_ref[...], scaled_ref[...], NT, preferred_element_type=F32)
    for q in range(chunks):
        put(row_out_refs, q, normed[q * CHUNK : (q + 1) * CHUNK, :])
    exchange(row_out_refs, row_in_refs, 3, 1, BEHIND)

    found = lax.dot_general(hot_ref[...], table_ref[...], NT, preferred_element_type=F32)
    inverse = (
        found[:, width : width + 1] + found[:, width + 1 : width + 2] + found[:, width + 2 : width + 3]
    )
    unit_ref[...] = found[:, :width] * (scale * inverse)
    inv_ref[...] = jnp.broadcast_to(inverse, (slots, 128))

    for n in range(2):
        wait_blocks(cot_in_refs[n], owners - 1, recv_sems.at[1 + n])
    sums = []
    total = jnp.zeros((1, width), F32)
    for q in range(chunks):
        span = slice(q * CHUNK, (q + 1) * CHUNK)
        product = get(cot_in_refs, q) * unit_ref[span, :]
        total += jnp.sum(product, axis=0, keepdims=True)
        sums.append(jnp.sum(product * multiplier, axis=1, keepdims=True))
    part_ref[...] = as_rows(sums)
    start_sum(part_ref, inner_ref, 10)
    wgp_ref[:, :width] = total
    wgp_ref[:, width:] = jnp.zeros((1, wide - width), F32)
    share(wgp_ref, wg1_ref, 5, inner_id, cores, beside)
    exchange(row_out_refs, row_in_refs, 3, BEHIND, owners)

    def second_step():
        wait_blocks(wg1_ref, cores - 1, recv_sems.at[5])
        wgs_ref[...] = jnp.sum(wg1_ref[...], axis=0)
        share(wgs_ref, wg2_ref, 6, height, heights, above)

    inner = cross(inner_ref, inner_sum_ref, inner_other_ref, 10, second_step)
    inner = as_columns(inner * (1.0 / (width * ring)))
    for q in range(chunks):
        span = slice(q * CHUNK, (q + 1) * CHUNK)
        left = get(cot_in_refs, q) * multiplier - unit_ref[span, :] * inner[:, q : q + 1]
        g_ref[span, :] = (scale * inv_ref[span, :1] * left).astype(BF16)

    grad_ref[...] = lax.dot_general(
        g_ref[...], hot_ref[...], TN, preferred_element_type=F32
    ).astype(BF16)

    wait_blocks(wg2_ref, heights - 1, recv_sems.at[6])
    wg_ref[...] = jnp.sum(wg2_ref[...], axis=0)
    for n in range(2):
        wait_blocks(row_in_refs[n], owners - 1, recv_sems.at[3 + n])
    for n, (ref, number) in enumerate(
        (
            (ask_ref, owners),
            (cot_out_refs[0], owners),
            (cot_out_refs[1], owners),
            (row_out_refs[0], owners),
            (row_out_refs[1], owners),
            (wg1_ref, cores),
            (wg2_ref, heights),
        )
    ):
        wait_blocks(ref, number - 1, send_sems.at[n])
    end_sum(square_ref, 7)
    end_sum(inner_ref, 10)


def body(mesh, token_ids, table, norm_weight, cotangent):
    groups, ring = mesh.shape["dp"], mesh.shape["mp"]
    owners = mesh.shape["section"] * groups
    vrows, width = table.shape
    count = token_ids.shape[0]
    cap = 2 * count // owners
    cores = 8
    heights = owners // cores
    slots = owners * cap
    chunks = slots // CHUNK
    wide = -(-width // 128) * 128
    operands = (token_ids.reshape(1, count), norm_weight, cotangent.T, table.T)
    full = width // 128 * 128
    blocks = (
        pltpu.VMEM((owners, cap, full), BF16),
        pltpu.VMEM((owners, cap // 2, 2 * (width - full)), BF16),
    )
    vmem = pl.BlockSpec(memory_space=pltpu.VMEM)
    hbm = pl.BlockSpec(memory_space=pltpu.HBM)
    block_shapes = tuple(jax.ShapeDtypeStruct(block.shape, BF16) for block in blocks)
    parts = pl.pallas_call(
        functools.partial(kernel, (groups, ring, cap, cores)),
        out_shape=(
            *block_shapes,
            jax.ShapeDtypeStruct((slots, count), BF16),
            jax.ShapeDtypeStruct((1, wide), F32),
            jax.ShapeDtypeStruct((width, vrows), BF16),
        ),
        in_specs=[hbm] * 4,
        out_specs=(vmem,) * 5,
        scratch_shapes=[
            pltpu.VMEM((1, count), jnp.int32),
            pltpu.VMEM((width,), F32),
            pltpu.VMEM((width + 16, vrows), BF16),
            pltpu.VMEM((width, count), BF16),
            pltpu.VMEM((owners, 1, 128), jnp.int32),
            pltpu.VMEM((owners, 1, 128), jnp.int32),
            blocks,
            blocks,
            blocks,
            pltpu.VMEM((slots, vrows), BF16),
            pltpu.VMEM((slots, width), F32),
            pltpu.VMEM((chunks, 128), F32),
            pltpu.VMEM((ring // 2, 1, -(-vrows // 128) * 128), F32),
            pltpu.VMEM((1, 1, -(-vrows // 128) * 128), F32),
            pltpu.VMEM((1, 1, -(-vrows // 128) * 128), F32),
            pltpu.VMEM((ring // 2, chunks, 128), F32),
            pltpu.VMEM((1, chunks, 128), F32),
            pltpu.VMEM((1, chunks, 128), F32),
            pltpu.VMEM((width, 128), F32),
            pltpu.VMEM((slots, 128), F32),
            pltpu.VMEM((width, vrows), BF16),
            pltpu.VMEM((1, -(-vrows // 128) * 128), F32),
            pltpu.VMEM((slots, width), BF16),
            pltpu.VMEM((1, wide), F32),
            pltpu.VMEM((cores, 1, wide), F32),
            pltpu.VMEM((1, wide), F32),
            pltpu.VMEM((heights, 1, wide), F32),
            pltpu.SemaphoreType.DMA((4,)),
            pltpu.SemaphoreType.DMA((13,)),
            pltpu.SemaphoreType.DMA((13,)),
        ],
        compiler_params=pltpu.CompilerParams(
            collective_id=0, has_side_effects=True, vmem_limit_bytes=32 * 1024 * 1024
        ),
    )(*(pltpu.with_memory_space_constraint(x, pltpu.HBM) for x in operands))
    normed, weight_grad, table_grad = pl.pallas_call(
        finish,
        out_shape=(
            jax.ShapeDtypeStruct((width, count), BF16),
            jax.ShapeDtypeStruct((width,), F32),
            jax.ShapeDtypeStruct((width, vrows), BF16),
        ),
        in_specs=[vmem] * 5,
        out_specs=(hbm,) * 3,
        scratch_shapes=[
            pltpu.VMEM((width, count), BF16),
            pltpu.VMEM((width,), F32),
            pltpu.SemaphoreType.DMA((3,)),
        ],
        compiler_params=pltpu.CompilerParams(vmem_limit_bytes=32 * 1024 * 1024),
    )(*parts)
    return normed.T, weight_grad, table_grad.T


def solution(mesh):
    placed = (P(("section", "dp")), P(("section", "dp"), "mp"), P("mp"), P(("section", "dp"), "mp"))
    return jax.shard_map(
        functools.partial(body, mesh),
        mesh=mesh,
        in_specs=placed,
        out_specs=(P(("section", "dp"), "mp"), P("mp"), P(("section", "dp"), "mp")),
        check_vma=False,
    )
```
